32 devices in a mesh: dp: 8 (over y, x, core), space: 4 (over z).
Axes of the slice: x: 2, y: 2, z: 4, core: 2. Of those that a mesh axis runs over, the one named last changes fastest.
Arguments:
- images: bfloat16 [8, 16, 128, 1024], P('dp', 'space'), may hold values from -18 to 18
- teacher: bfloat16 [8, 16, 128, 1024], P('dp', 'space'), may hold values from 0 to 400
- w_reduce: bfloat16 [1024, 256], replicated, may hold values from -0.1875 to 0.1875
- w_spatial: bfloat16 [3, 3, 256, 256], replicated, may hold values from -0.125 to 0.125
- w_expand: bfloat16 [256, 1024], replicated, may hold values from -0.375 to 0.375
- partners: int32 [2, 8], replicated, may hold values from 0 to 7, as said below
Outputs:
- distill_loss: float32 [], replicated
- grad_images: bfloat16 [8, 16, 128, 1024], P('dp', 'space')
- grad_reduce: float32 [8, 1024, 256], P('dp', 'space')
- grad_spatial: float32 [8, 3, 3, 256, 256], P('dp', None, None, None, 'space')
- grad_expand: float32 [8, 256, 1024], P('dp', None, 'space')
The draws below stay inside these ranges and needn't reach their ends.
Inputs may be any that keep to these rules, and one draw needn't show every extreme that they name: partners[r, i] = i XOR m_r for a round value m_r of 1 to 7, the m_r distinct over rounds; so each round pairs the images and partners[r, partners[r, i]] = i.
All inputs are finite; a program needn't handle non-finite values.
Results may differ from the reference program's by a relative error of at most 0.019.
The reference program's roundings to bfloat16 on the way count: a program that leaves them out, or rounds other values in their place, can miss the bound.
Values may be sent and summed in bfloat16 or wider, within the bound.
A program may use at most 64 MiB of HBM per device.

```python
import math
import jax
import jax.numpy as jnp
from jax import lax

C = 1024
MID = 256
COLS = 128
ROWS_DEV = 4
ROUNDS = 2
ROWS = 16
IMAGES = 8
ELEMS = 2097152


def draw_images(key, part):
    keys = jax.random.split(jax.random.fold_in(key, 5), 2)
    shape = (IMAGES, ROWS, COLS, C)
    base = jnp.clip(jax.random.normal(keys[0], shape, jnp.float32), -6.0, 6.0)
    band_count = ROWS // ROWS_DEV
    heavy = jax.random.randint(keys[1], (IMAGES, 1), 0, band_count).astype(jnp.int32)
    band_of_row = jnp.arange(ROWS, dtype=jnp.int32) // ROWS_DEV
    factor = jnp.where(band_of_row[None, :] == heavy, 3.0, 1.0).reshape(IMAGES, ROWS, 1, 1)
    return (base * factor).astype(jnp.bfloat16)


def draw_teacher(key, part):
    keys = jax.random.split(jax.random.fold_in(key, 11), 7)
    shape = (IMAGES, ROWS, COLS, C)
    noise = jnp.clip(jax.random.normal(keys[0], shape, jnp.float32), -6.0, 6.0) * 0.6
    common = jnp.clip(jax.random.normal(keys[4], (1, ROWS, COLS, C), jnp.float32), -4.0, 4.0)
    offset = jnp.clip(jax.random.normal(keys[1], (IMAGES, 1, 1, C), jnp.float32), -3.0, 3.0) * 0.5
    amount = jax.random.uniform(keys[5], (IMAGES, 1, 1, 1), jnp.float32, -2.0, 2.0)
    steps = (jnp.arange(COLS, dtype=jnp.float32) / max(COLS - 1, 1)).reshape(1, 1, COLS, 1)
    rising = jax.random.uniform(keys[6], (IMAGES, 1, 1, 1), jnp.float32) < 0.5
    ramp = jnp.exp(math.log(3.0) * jnp.where(rising, steps, 1.0 - steps))
    scale = jnp.exp(jax.random.uniform(keys[2], (1, 1, 1, C), jnp.float32) * math.log(10.0))
    band = jnp.exp(jax.random.uniform(keys[3], (IMAGES, ROWS, 1, 1), jnp.float32) * math.log(4.0))
    phase = jax.random.randint(jax.random.fold_in(key, 31), (IMAGES, 1, 1, 1), 0, 8).astype(jnp.int32)
    diag = (jnp.arange(ROWS, dtype=jnp.int32)[:, None] + jnp.arange(COLS, dtype=jnp.int32)[None, :]) % 8
    lattice = jnp.where(diag[None, :, :, None] == phase, 4.0, 1.0)
    values = lattice * scale * band * ramp * jax.nn.relu(offset + amount * common + noise)
    return jnp.clip(values, 0.0, 400.0).astype(jnp.bfloat16)


def draw_partners(key, part):
    order = jax.random.permutation(jax.random.fold_in(key, 23), IMAGES - 1)
    masks = order[:ROUNDS].astype(jnp.int32) + 1
    ranks = jnp.arange(IMAGES, dtype=jnp.int32)
    return jnp.bitwise_xor(ranks[None, :], masks[:, None]).astype(jnp.int32)


def centred(rng, shape, scale, reach, kind=jnp.bfloat16):
    values = jax.random.normal(rng, shape, jnp.float32) * scale
    return jnp.minimum(jnp.maximum(values, -reach), reach).astype(kind)


def setup_inputs(seed: int = 0) -> dict:
    key_of = jax.random.split(jax.random.key(seed), 7)
    return {
        "images": draw_images(jax.random.fold_in(key_of[6], 71), 0),
        "teacher": draw_teacher(jax.random.fold_in(key_of[6], 71), 0),
        "w_reduce": centred(key_of[2], (C, MID), C ** -0.5, 0.1875),
        "w_spatial": centred(key_of[3], (3, 3, MID, MID), (9 * MID) ** -0.5, 0.125),
        "w_expand": centred(key_of[4], (MID, C), MID ** -0.5, 0.375),
        "partners": draw_partners(jax.random.fold_in(key_of[6], 71), 0),
    }


def conv_taps(padded, weights, row_count, col_count, flipped):
    channels = padded.shape[-1]
    summed = None
    for row_step in range(3):
        for col_step in range(3):
            if flipped:
                window = padded[:, 2 - row_step:2 - row_step + row_count, 2 - col_step:2 - col_step + col_count, :]
                tap = weights[row_step, col_step].T
            else:
                window = padded[:, row_step:row_step + row_count, col_step:col_step + col_count, :]
                tap = weights[row_step, col_step]
            part_sum = jnp.dot(window.reshape(-1, channels), tap, preferred_element_type=jnp.float32)
            summed = part_sum if summed is None else summed + part_sum
    return summed

def gram_rows(features, partners):
    flat = features.reshape(features.shape[0], -1).astype(jnp.float32)
    columns = [lax.optimization_barrier(jnp.sum(flat * flat, axis=1))]
    for round_index in range(partners.shape[0]):
        columns.append(lax.optimization_barrier(jnp.sum(flat * flat[partners[round_index]], axis=1)))
    return jnp.stack(columns, axis=1)

def per_image(left, right, batch):
    left_img = left.reshape(batch, -1, left.shape[-1])
    right_img = right.reshape(batch, -1, right.shape[-1])
    return jnp.stack([jnp.dot(left_img[index].T, right_img[index], preferred_element_type=jnp.float32) for index in range(batch)])

def reference(images, teacher, w_reduce, w_spatial, w_expand, partners):
    batch, row_count, col_count, channels = images.shape
    hidden = w_reduce.shape[1]
    flat_x = images.reshape(-1, channels)
    h_one = jax.nn.relu(jnp.dot(flat_x, w_reduce, preferred_element_type=jnp.float32)).astype(jnp.bfloat16)
    pad_one = jnp.pad(h_one.reshape(batch, row_count, col_count, hidden), ((0, 0), (1, 1), (1, 1), (0, 0)))
    h_two = jax.nn.relu(conv_taps(pad_one, w_spatial, row_count, col_count, False)).astype(jnp.bfloat16)
    pre_act = jnp.dot(h_two, w_expand, preferred_element_type=jnp.float32) + flat_x.astype(jnp.float32)
    student = jax.nn.relu(pre_act).astype(jnp.bfloat16)
    student_img = student.reshape(batch, -1)
    v_student = gram_rows(student_img, partners)
    v_teacher = gram_rows(teacher.reshape(batch, -1), partners)
    nu_student = jnp.sqrt(lax.optimization_barrier(jnp.sum(v_student * v_student, axis=1, keepdims=True)) + 1e-06)
    nu_teacher = jnp.sqrt(lax.optimization_barrier(jnp.sum(v_teacher * v_teacher, axis=1, keepdims=True)) + 1e-06)
    n_student = v_student / nu_student
    n_teacher = v_teacher / nu_teacher
    diff = n_student - n_teacher
    distill_loss = jnp.sum(diff * diff)
    err = 2.0 * diff
    coefs = (err - lax.optimization_barrier(jnp.sum(err * n_student, axis=1, keepdims=True)) * n_student) / nu_student
    student_f = student_img.astype(jnp.float32)
    summed = 2.0 * coefs[:, 0:1] * student_f
    for round_index in range(partners.shape[0]):
        partner = partners[round_index]
        weight = coefs[:, round_index + 1] + coefs[partner, round_index + 1]
        summed = summed + weight[:, None] * student_f[partner]
    grad_student = (ELEMS * summed).astype(jnp.bfloat16).reshape(-1, channels)
    g_pre = jnp.where(student > 0, grad_student, jnp.zeros_like(grad_student))
    grad_expand = per_image(h_two, g_pre, batch)
    back_two = jnp.dot(g_pre, w_expand.T, preferred_element_type=jnp.float32)
    g_two = jnp.where(h_two > 0, back_two, 0.0).astype(jnp.bfloat16)
    g_two_img = g_two.reshape(batch, row_count, col_count, hidden)
    tap_grads = []
    for row_step in range(3):
        tap_row = []
        for col_step in range(3):
            window = pad_one[:, row_step:row_step + row_count, col_step:col_step + col_count, :].reshape(-1, hidden)
            tap_row.append(per_image(window, g_two, batch))
        tap_grads.append(jnp.stack(tap_row, axis=1))
    grad_spatial = jnp.stack(tap_grads, axis=1)
    pad_grad = jnp.pad(g_two_img, ((0, 0), (1, 1), (1, 1), (0, 0)))
    back_one = conv_taps(pad_grad, w_spatial, row_count, col_count, True)
    g_one = jnp.where(h_one > 0, back_one, 0.0).astype(jnp.bfloat16)
    grad_reduce = per_image(flat_x, g_one, batch)
    grad_images = (g_pre.astype(jnp.float32) + jnp.dot(g_one, w_reduce.T, preferred_element_type=jnp.float32)).astype(jnp.bfloat16)
    grad_images = grad_images.reshape(batch, row_count, col_count, channels)
    return (distill_loss, grad_images, grad_reduce, grad_spatial, grad_expand)
```

```python
import functools

import jax
import jax.numpy as jnp
from jax import lax
from jax.experimental import pallas as pl
from jax.experimental.pallas import tpu as pltpu
from jax.sharding import PartitionSpec as P

MESH = pl.DeviceIdType.MESH
F32 = jnp.float32
BF16 = jnp.bfloat16


def mm(a, b, ca=1, cb=0):
    return lax.dot_general(a, b, (((ca,), (cb,)), ((), ())), preferred_element_type=F32)


def kernel(
    dims, part, x, t, wr, ws, we,
    loss_o, gi_o, gr_o, gs_o, ge_o,
    h1, h2, st, patch, g2, xt, h2t, up, down, up2, down2,
    tcut, scut, gcut, gpre, gram, slots, zsend, zslots, coef,
    grp, gsp, gep, grr, gsr, ger,
    t_send, t_recv, s_send, s_recv, g_send, g_recv, v_send, v_recv,
    z_send, z_recv, e_send, e_recv, r_send, r_recv,
):
    dp, sp, rows, cols, elems = dims
    chans, mid = wr.shape
    pixels = rows * cols
    span = pixels // dp
    me = lax.axis_index("dp")
    my = lax.axis_index("space")

    def dp_peer(shift):
        return lax.rem(me + shift, dp)

    def sp_peer(shift):
        return lax.rem(my + shift, sp)

    def remote(src, dst, send, recv, where):
        return pltpu.make_async_remote_copy(
            src_ref=src, dst_ref=dst, send_sem=send, recv_sem=recv,
            device_id=where, device_id_type=MESH,
        )

    up[...] = jnp.zeros_like(up)
    down[...] = jnp.zeros_like(down)
    up2[...] = jnp.zeros_like(up2)
    down2[...] = jnp.zeros_like(down2)

    barrier = pltpu.get_barrier_semaphore()
    for shift in range(1, dp):
        pl.semaphore_signal(
            barrier, inc=1, device_id={"dp": dp_peer(shift)}, device_id_type=MESH
        )
    for shift in range(1, sp):
        pl.semaphore_signal(
            barrier, inc=1, device_id={"space": sp_peer(shift)}, device_id_type=MESH
        )
    pl.semaphore_wait(barrier, dp + sp - 2)

    def cut_copy(src, dst, send, recv, shift):
        peer = dp_peer(shift)
        return remote(
            src.at[pl.ds(pl.multiple_of(peer * span, span), span)],
            dst.at[me], send.at[shift - 1], recv.at[shift - 1], {"dp": peer},
        )

    def cut_arrival(src, dst, send, recv, shift):
        origin = lax.rem(me + dp - shift, dp)
        return remote(
            src.at[pl.ds(0, span)], dst.at[origin],
            send.at[shift - 1], recv.at[shift - 1], {"dp": origin},
        )

    mine = pl.ds(pl.multiple_of(me * span, span), span)
    for shift in range(1, dp):
        cut_copy(t, tcut, t_send, t_recv, shift).start()
    tcut[me] = t[mine, :]

    def edges(src, above, below, base, act):
        first, last = src.at[pl.ds(0, cols)], src.at[pl.ds(pixels - cols, cols)]

        def move(part_rows, dst, slot, peer):
            return remote(
                part_rows, dst, e_send.at[slot], e_recv.at[slot], {"space": peer}
            )

        @pl.when(my > 0)
        def _():
            if act == "start":
                move(first, below, base, my - 1).start()
            elif act == "recv":
                move(first, above, base + 1, my - 1).wait_recv()
            else:
                move(first, below, base, my - 1).wait_send()

        @pl.when(my < sp - 1)
        def _():
            if act == "start":
                move(last, above, base + 1, my + 1).start()
            elif act == "recv":
                move(last, below, base, my + 1).wait_recv()
            else:
                move(last, above, base + 1, my + 1).wait_send()

    column = lax.broadcasted_iota(jnp.int32, (cols, mid), 0)

    def place(value, row):
        wide = value.astype(F32)
        left = jnp.where(column == 0, 0.0, pltpu.roll(wide, 1, 0)).astype(BF16)
        right = jnp.where(column == cols - 1, 0.0, pltpu.roll(wide, cols - 1, 0)).astype(BF16)
        for a in range(3):
            to = row - a + 1
            if 0 <= to < rows:
                for b, piece in enumerate((left, value, right)):
                    tap = a * 3 + b
                    patch[to * cols:(to + 1) * cols, tap * mid:(tap + 1) * mid] = piece

    h1[...] = jnp.maximum(mm(x[...], wr[...]), 0.0).astype(BF16)
    edges(h1, up, down, 0, "start")
    for row in range(rows):
        place(h1[row * cols:(row + 1) * cols, :], row)
    edges(h1, up, down, 0, "recv")
    place(up[...], -1)
    place(down[...], rows)
    h2[...] = jnp.maximum(mm(patch[...], ws[...]), 0.0).astype(BF16)
    for row in range(rows):
        at = slice(row * cols, (row + 1) * cols)
        st[at, :] = jnp.maximum(mm(h2[at, :], we[...]) + x[at, :].astype(F32), 0.0).astype(BF16)
    for shift in range(1, dp):
        cut_copy(st, scut, s_send, s_recv, shift).start()
    scut[me] = st[mine, :]

    lane = lax.broadcasted_iota(jnp.int32, (1, 128), 1)

    def gram_rows(cut, first):
        def one(i, carry):
            others = [part[0, i], part[1, i]]
            sums = [jnp.zeros((8, 128), F32) for _ in range(3)]
            for block in range(chans // 128):
                at = slice(block * 128, (block + 1) * 128)
                own = cut[i, :, at].astype(F32)
                for j, right in enumerate(
                    (own, cut[others[0], :, at].astype(F32), cut[others[1], :, at].astype(F32))
                ):
                    sums[j] = sums[j] + jnp.sum((own * right).reshape(span // 8, 8, 128), axis=0)
            line = jnp.zeros((1, 128), F32)
            for j in range(3):
                total = jnp.sum(jnp.sum(sums[j], axis=0, keepdims=True), axis=1, keepdims=True)
                line = jnp.where(lane == first + j, total, line)
            if first:
                gram[pl.ds(i, 1), :] = jnp.where(lane >= first, line, gram[pl.ds(i, 1), :])
            else:
                gram[pl.ds(i, 1), :] = line
            return carry

        lax.fori_loop(0, dp, one, 0)

    for shift in range(1, dp):
        cut_arrival(t, tcut, t_send, t_recv, shift).wait_recv()
    gram_rows(tcut, 0)
    xt[...] = x[...].T
    h2t[...] = h2[...].T
    for shift in range(1, dp):
        cut_arrival(st, scut, s_send, s_recv, shift).wait_recv()
    gram_rows(scut, 3)

    def gram_copy(shift):
        return remote(
            gram, slots.at[me], v_send.at[shift - 1], v_recv.at[shift - 1],
            {"dp": dp_peer(shift)},
        )

    for shift in range(1, dp):
        gram_copy(shift).start()
    slots[me] = gram[...]
    for shift in range(1, dp):
        origin = lax.rem(me + dp - shift, dp)
        remote(
            gram, slots.at[origin], v_send.at[shift - 1], v_recv.at[shift - 1], {"dp": origin}
        ).wait_recv()
    total = slots[0]
    for k in range(1, dp):
        total = total + slots[k]
    zsend[...] = total

    def sum_copy(shift):
        return remote(
            zsend, zslots.at[my], z_send.at[shift - 1], z_recv.at[shift - 1],
            {"space": sp_peer(shift)},
        )

    for shift in range(1, sp):
        sum_copy(shift).start()
    zslots[my] = total
    for shift in range(1, sp):
        origin = lax.rem(my + sp - shift, sp)
        remote(
            zsend, zslots.at[origin], z_send.at[shift - 1], z_recv.at[shift - 1],
            {"space": origin},
        ).wait_recv()
    total = zslots[0]
    for k in range(1, sp):
        total = total + zslots[k]
    lanes = lax.broadcasted_iota(jnp.int32, (dp, 128), 1)

    def spread(j):
        one = jnp.sum(jnp.where(lanes == j, total, 0.0), axis=1, keepdims=True)
        return jnp.broadcast_to(one, (dp, 128))

    v_t = [spread(j) for j in range(3)]
    v_s = [spread(3 + j) for j in range(3)]
    nu_t = jnp.sqrt(v_t[0] * v_t[0] + v_t[1] * v_t[1] + v_t[2] * v_t[2] + 1e-06)
    nu_s = jnp.sqrt(v_s[0] * v_s[0] + v_s[1] * v_s[1] + v_s[2] * v_s[2] + 1e-06)
    n_s = [v / nu_s for v in v_s]
    diff = [a - b / nu_t for a, b in zip(n_s, v_t)]
    loss = diff[0] * diff[0] + diff[1] * diff[1] + diff[2] * diff[2]
    loss_o[...] = jnp.sum(loss, axis=0, keepdims=True)
    err = [2.0 * d for d in diff]
    along = err[0] * n_s[0] + err[1] * n_s[1] + err[2] * n_s[2]
    for j in range(3):
        coef[j] = (err[j] - along * n_s[j]) / nu_s

    def grad_slice(i):
        one, two = part[0, i], part[1, i]
        weights = (
            2.0 * coef[0, pl.ds(i, 1), :],
            coef[1, pl.ds(i, 1), :] + coef[1, pl.ds(one, 1), :],
            coef[2, pl.ds(i, 1), :] + coef[2, pl.ds(two, 1), :],
        )
        for block in range(chans // 128):
            at = slice(block * 128, (block + 1) * 128)
            own = scut[i, :, at].astype(F32)
            summed = weights[0] * own
            summed = summed + weights[1] * scut[one, :, at].astype(F32)
            summed = summed + weights[2] * scut[two, :, at].astype(F32)
            gcut[i, :, at] = jnp.where(own > 0, elems * summed, 0.0).astype(BF16)

    def grad_copy(shift):
        peer = dp_peer(shift)
        return remote(
            gcut.at[peer], gpre.at[mine], g_send.at[shift - 1], g_recv.at[shift - 1],
            {"dp": peer},
        )

    def send_slice(shift, carry):
        grad_slice(dp_peer(shift))
        grad_copy(shift).start()
        return carry

    lax.fori_loop(1, dp, send_slice, 0)
    grad_slice(me)
    gpre[mine, :] = gcut[me]
    for shift in range(1, dp):
        origin = lax.rem(me + dp - shift, dp)
        remote(
            gcut.at[origin], gpre.at[pl.ds(pl.multiple_of(origin * span, span), span)],
            g_send.at[shift - 1], g_recv.at[shift - 1], {"dp": origin},
        ).wait_recv()

    g2[...] = jnp.where(h2[...] > 0, mm(gpre[...], we[...], 1, 1), 0.0).astype(BF16)
    edges(g2, up2, down2, 2, "start")

    width = chans // sp
    depth = mid // sp

    def ge_copy(shift):
        return remote(
            gep.at[sp_peer(shift)], ger.at[shift - 1], r_send.at[0, shift - 1],
            r_recv.at[0, shift - 1], {"space": sp_peer(shift)},
        )

    def gs_copy(shift):
        peer = sp_peer(shift)
        return remote(
            gsp.at[pl.ds(pl.multiple_of(peer * depth, depth), depth)], gsr.at[shift - 1],
            r_send.at[1, shift - 1], r_recv.at[1, shift - 1], {"space": peer},
        )

    def gr_copy(shift):
        peer = sp_peer(shift)
        return remote(
            grp.at[pl.ds(pl.multiple_of(peer * width, width), width)], grr.at[shift - 1],
            r_send.at[2, shift - 1], r_recv.at[2, shift - 1], {"space": peer},
        )

    for k in range(sp):
        gep[k] = mm(h2t[...], gpre[:, k * width:(k + 1) * width]).astype(BF16)
    for shift in range(1, sp):
        ge_copy(shift).start()
    g2t = g2[...].T
    for tap in range(9):
        at = slice(tap * mid, (tap + 1) * mid)
        gsp[:, at] = mm(g2t, patch[:, at]).astype(BF16)
    for shift in range(1, sp):
        gs_copy(shift).start()

    for row in range(rows):
        place(g2[row * cols:(row + 1) * cols, :], row)
    edges(g2, up2, down2, 2, "recv")
    place(up2[...], -1)
    place(down2[...], rows)
    back = None
    for tap in range(9):
        flip = 8 - tap
        term = mm(
            patch[:, tap * mid:(tap + 1) * mid], ws[flip * mid:(flip + 1) * mid, :], 1, 1
        )
        back = term if back is None else back + term
    edges(h1, up, down, 0, "send")
    g1 = jnp.where(h1[...] > 0, back, 0.0).astype(BF16)
    grp[...] = mm(xt[...], g1).astype(BF16)
    for shift in range(1, sp):
        gr_copy(shift).start()
    h1[...] = g1
    for row in range(rows):
        at = slice(row * cols, (row + 1) * cols)
        gi_o[at, :] = (gpre[at, :].astype(F32) + mm(h1[at, :], wr[...], 1, 1)).astype(BF16)

    for shift in range(1, sp):
        ge_copy(shift).wait_recv()
    ge = gep[my].astype(F32)
    for k in range(sp - 1):
        ge = ge + ger[k].astype(F32)
    ge_o[...] = ge
    for shift in range(1, sp):
        gs_copy(shift).wait_recv()
    at_rows = pl.ds(pl.multiple_of(my * depth, depth), depth)
    for tap in range(9):
        at = slice(tap * mid, (tap + 1) * mid)
        gs = gsp[at_rows, at].astype(F32)
        for k in range(sp - 1):
            gs = gs + gsr[k, :, at].astype(F32)
        gs_o[tap] = gs
    for shift in range(1, sp):
        gr_copy(shift).wait_recv()
    gr = grp[pl.ds(pl.multiple_of(my * width, width), width), :].astype(F32)
    for k in range(sp - 1):
        gr = gr + grr[k].astype(F32)
    gr_o[...] = gr

    for shift in range(1, dp):
        cut_copy(t, tcut, t_send, t_recv, shift).wait_send()
        cut_copy(st, scut, s_send, s_recv, shift).wait_send()
        gram_copy(shift).wait_send()
        grad_copy(shift).wait_send()
    edges(g2, up2, down2, 2, "send")
    for shift in range(1, sp):
        sum_copy(shift).wait_send()
        ge_copy(shift).wait_send()
        gs_copy(shift).wait_send()
        gr_copy(shift).wait_send()


def body(images, teacher, w_reduce, w_spatial, w_expand, partners):
    dp, sp = lax.axis_size("dp"), lax.axis_size("space")
    _, rows, cols, chans = images.shape
    mid = w_reduce.shape[1]
    pixels = rows * cols
    span, width, depth = pixels // dp, chans // sp, mid // sp
    elems = float(rows * sp * cols * chans)
    vmem = pl.BlockSpec(memory_space=pltpu.VMEM)
    dma = pltpu.SemaphoreType.DMA
    loss, gi, gr, gs, ge = pl.pallas_call(
        functools.partial(kernel, (dp, sp, rows, cols, elems)),
        out_shape=(
            jax.ShapeDtypeStruct((1, 128), F32),
            jax.ShapeDtypeStruct((pixels, chans), BF16),
            jax.ShapeDtypeStruct((width, mid), F32),
            jax.ShapeDtypeStruct((9, depth, mid), F32),
            jax.ShapeDtypeStruct((mid, width), F32),
        ),
        in_specs=[pl.BlockSpec(memory_space=pltpu.SMEM)] + [vmem] * 5,
        out_specs=(vmem,) * 5,
        scratch_shapes=[
            pltpu.VMEM((pixels, mid), BF16),
            pltpu.VMEM((pixels, mid), BF16),
            pltpu.VMEM((pixels, chans), BF16),
            pltpu.VMEM((pixels, 9 * mid), BF16),
            pltpu.VMEM((pixels, mid), BF16),
            pltpu.VMEM((chans, pixels), BF16),
            pltpu.VMEM((mid, pixels), BF16),
            pltpu.VMEM((cols, mid), BF16),
            pltpu.VMEM((cols, mid), BF16),
            pltpu.VMEM((cols, mid), BF16),
            pltpu.VMEM((cols, mid), BF16),
            pltpu.VMEM((dp, span, chans), BF16),
            pltpu.VMEM((dp, span, chans), BF16),
            pltpu.VMEM((dp, span, chans), BF16),
            pltpu.VMEM((pixels, chans), BF16),
            pltpu.VMEM((dp, 128), F32),
            pltpu.VMEM((dp, dp, 128), F32),
            pltpu.VMEM((dp, 128), F32),
            pltpu.VMEM((sp, dp, 128), F32),
            pltpu.VMEM((3, dp, 128), F32),
            pltpu.VMEM((chans, mid), BF16),
            pltpu.VMEM((mid, 9 * mid), BF16),
            pltpu.VMEM((sp, mid, width), BF16),
            pltpu.VMEM((sp - 1, width, mid), BF16),
            pltpu.VMEM((sp - 1, depth, 9 * mid), BF16),
            pltpu.VMEM((sp - 1, mid, width), BF16),
            dma((dp - 1,)), dma((dp - 1,)), dma((dp - 1,)), dma((dp - 1,)),
            dma((dp - 1,)), dma((dp - 1,)), dma((dp - 1,)), dma((dp - 1,)),
            dma((sp - 1,)), dma((sp - 1,)), dma((4,)), dma((4,)),
            dma((3, sp - 1)), dma((3, sp - 1)),
        ],
        compiler_params=pltpu.CompilerParams(
            collective_id=0, has_side_effects=True, vmem_limit_bytes=48 * 1024 * 1024
        ),
        name="distill",
    )(
        partners,
        images.reshape(pixels, chans),
        teacher.reshape(pixels, chans),
        w_reduce,
        w_spatial.reshape(9 * mid, mid),
        w_expand,
    )
    return (
        loss[0, 0],
        gi.reshape(images.shape),
        gr[None],
        gs.reshape(1, 3, 3, depth, mid).transpose(0, 1, 2, 4, 3),
        ge[None],
    )


def solution(mesh):
    return jax.shard_map(
        body,
        mesh=mesh,
        in_specs=(P("dp", "space", None, None), P("dp", "space", None, None), P(), P(), P(), P()),
        out_specs=(
            P(),
            P("dp", "space", None, None),
            P("dp", "space", None),
            P("dp", None, None, None, "space"),
            P("dp", None, "space"),
        ),
        check_vma=False,
    )
```

```python
import functools

import jax
import jax.numpy as jnp
from jax import lax
from jax.experimental import pallas as pl
from jax.experimental.pallas import tpu as pltpu
from jax.sharding import PartitionSpec as P

MESH = pl.DeviceIdType.MESH
F32 = jnp.float32
BF16 = jnp.bfloat16


def mm(a, b, ca=1, cb=0):
    return lax.dot_general(a, b, (((ca,), (cb,)), ((), ())), preferred_element_type=F32)


def kernel(
    dims, part, x_hbm, t, wr_hbm, ws_hbm, we_hbm,
    loss_o, gi_o, gr_o, gs_o, ge_o,
    x, wr, ws, we, h1, g1, h1f, g2t, g2f, h2, st, patch, g2, xt, h2t, up, down, up2, down2,
    tcut, scut, gcut, gpre, gram, slots, zsend, zslots, coef,
    grp, gep, grr, ger,
    t_send, t_recv, s_send, s_recv, g_send, g_recv, v_send, v_recv,
    z_send, z_recv, e_send, e_recv, r_send, r_recv, l_sem,
):
    dp, sp, rows, cols, elems = dims
    chans, mid = wr_hbm.shape
    pixels = rows * cols
    span = pixels // dp
    me = lax.axis_index("dp")
    my = lax.axis_index("space")

    def dp_peer(shift):
        return lax.rem(me + shift, dp)

    def sp_peer(shift):
        return lax.rem(my + shift, sp)

    def remote(src, dst, send, recv, where):
        return pltpu.make_async_remote_copy(
            src_ref=src, dst_ref=dst, send_sem=send, recv_sem=recv,
            device_id=where, device_id_type=MESH,
        )

    loads = [
        pltpu.make_async_copy(src, dst, l_sem.at[k])
        for k, (src, dst) in enumerate(((x_hbm, x), (wr_hbm, wr), (ws_hbm, ws), (we_hbm, we)))
    ]
    for load in loads:
        load.start()
    up[...] = jnp.zeros_like(up)
    down[...] = jnp.zeros_like(down)
    up2[...] = jnp.zeros_like(up2)
    down2[...] = jnp.zeros_like(down2)

    barrier = pltpu.get_barrier_semaphore()
    for shift in range(1, dp):
        pl.semaphore_signal(
            barrier, inc=1, device_id={"dp": dp_peer(shift)}, device_id_type=MESH
        )
    for shift in range(1, sp):
        pl.semaphore_signal(
            barrier, inc=1, device_id={"space": sp_peer(shift)}, device_id_type=MESH
        )
    pl.semaphore_wait(barrier, dp + sp - 2)

    def cut_copy(src, dst, send, recv, shift):
        peer = dp_peer(shift)
        return remote(
            src.at[pl.ds(pl.multiple_of(peer * span, span), span)],
            dst.at[me], send.at[shift - 1], recv.at[shift - 1], {"dp": peer},
        )

    def cut_arrival(src, dst, send, recv, shift):
        origin = lax.rem(me + dp - shift, dp)
        return remote(
            src.at[pl.ds(0, span)], dst.at[origin],
            send.at[shift - 1], recv.at[shift - 1], {"dp": origin},
        )

    mine = pl.ds(pl.multiple_of(me * span, span), span)
    for shift in range(1, dp):
        cut_copy(t, tcut, t_send, t_recv, shift).start()
    own_cut = pltpu.make_async_copy(t.at[mine], tcut.at[me], l_sem.at[4])
    own_cut.start()

    def edges(src, above, below, base, act):
        first, last = src.at[pl.ds(0, cols)], src.at[pl.ds(pixels - cols, cols)]

        def move(part_rows, dst, slot, peer):
            return remote(
                part_rows, dst, e_send.at[slot], e_recv.at[slot], {"space": peer}
            )

        @pl.when(my > 0)
        def _():
            if act == "start":
                move(first, below, base, my - 1).start()
            elif act == "recv":
                move(first, above, base + 1, my - 1).wait_recv()
            else:
                move(first, below, base, my - 1).wait_send()

        @pl.when(my < sp - 1)
        def _():
            if act == "start":
                move(last, above, base + 1, my + 1).start()
            elif act == "recv":
                move(last, below, base, my + 1).wait_recv()
            else:
                move(last, above, base + 1, my + 1).wait_send()

    column = lax.broadcasted_iota(jnp.int32, (cols, mid), 0)

    def place(value, row):
        wide = value.astype(F32)
        left = jnp.where(column == 0, 0.0, pltpu.roll(wide, 1, 0)).astype(BF16)
        right = jnp.where(column == cols - 1, 0.0, pltpu.roll(wide, cols - 1, 0)).astype(BF16)
        for a in range(3):
            to = row - a + 1
            if 0 <= to < rows:
                for b, piece in enumerate((left, value, right)):
                    tap = a * 3 + b
                    patch[to * cols:(to + 1) * cols, tap * mid:(tap + 1) * mid] = piece

    depth = mid // sp

    def h1_copy(shift):
        return remote(
            h1, h1f.at[pl.ds(pl.multiple_of(my * pixels, pixels), pixels)],
            r_send.at[1, shift - 1], r_recv.at[1, shift - 1], {"space": sp_peer(shift)},
        )

    def h1_arrival(shift):
        origin = lax.rem(my + sp - shift, sp)
        return remote(
            h1, h1f.at[pl.ds(pl.multiple_of(origin * pixels, pixels), pixels)],
            r_send.at[1, shift - 1], r_recv.at[1, shift - 1], {"space": origin},
        )

    def g2_copy(shift):
        peer = sp_peer(shift)
        return remote(
            g2t.at[pl.ds(pl.multiple_of(peer * depth, depth), depth)], g2f.at[my],
            r_send.at[3, shift - 1], r_recv.at[3, shift - 1], {"space": peer},
        )

    def g2_arrival(shift):
        origin = lax.rem(my + sp - shift, sp)
        return remote(
            g2t.at[pl.ds(0, depth)], g2f.at[origin],
            r_send.at[3, shift - 1], r_recv.at[3, shift - 1], {"space": origin},
        )

    loads[0].wait()
    loads[1].wait()
    h1[...] = jnp.maximum(mm(x[...], wr[...]), 0.0).astype(BF16)
    edges(h1, up, down, 0, "start")
    for shift in range(1, sp):
        h1_copy(shift).start()
    h1f[pl.ds(pl.multiple_of(my * pixels, pixels), pixels), :] = h1[...]
    for row in range(rows):
        place(h1[row * cols:(row + 1) * cols, :], row)
    edges(h1, up, down, 0, "recv")
    place(up[...], -1)
    place(down[...], rows)
    loads[2].wait()
    loads[3].wait()
    h2[...] = jnp.maximum(mm(patch[...], ws[...]), 0.0).astype(BF16)
    for row in range(rows):
        at = slice(row * cols, (row + 1) * cols)
        st[at, :] = jnp.maximum(mm(h2[at, :], we[...]) + x[at, :].astype(F32), 0.0).astype(BF16)
    for shift in range(1, dp):
        cut_copy(st, scut, s_send, s_recv, shift).start()
    scut[me] = st[mine, :]

    lane = lax.broadcasted_iota(jnp.int32, (1, 128), 1)

    def gram_rows(cut, first):
        def one(i, carry):
            others = [part[0, i], part[1, i]]
            sums = [jnp.zeros((8, 128), F32) for _ in range(3)]
            for block in range(chans // 128):
                at = slice(block * 128, (block + 1) * 128)
                own = cut[i, :, at].astype(F32)
                for j, right in enumerate(
                    (own, cut[others[0], :, at].astype(F32), cut[others[1], :, at].astype(F32))
                ):
                    sums[j] = sums[j] + jnp.sum((own * right).reshape(span // 8, 8, 128), axis=0)
            line = jnp.zeros((1, 128), F32)
            for j in range(3):
                total = jnp.sum(jnp.sum(sums[j], axis=0, keepdims=True), axis=1, keepdims=True)
                line = jnp.where(lane == first + j, total, line)
            if first:
                gram[pl.ds(i, 1), :] = jnp.where(lane >= first, line, gram[pl.ds(i, 1), :])
            else:
                gram[pl.ds(i, 1), :] = line
            return carry

        lax.fori_loop(0, dp, one, 0)

    for shift in range(1, dp):
        cut_arrival(t, tcut, t_send, t_recv, shift).wait_recv()
    own_cut.wait()
    gram_rows(tcut, 0)
    xt[...] = x[...].T
    h2t[...] = h2[...].T
    for shift in range(1, dp):
        cut_arrival(st, scut, s_send, s_recv, shift).wait_recv()
    gram_rows(scut, 3)

    def gram_copy(shift):
        return remote(
            gram, slots.at[me], v_send.at[shift - 1], v_recv.at[shift - 1],
            {"dp": dp_peer(shift)},
        )

    for shift in range(1, dp):
        gram_copy(shift).start()
    slots[me] = gram[...]
    for shift in range(1, dp):
        origin = lax.rem(me + dp - shift, dp)
        remote(
            gram, slots.at[origin], v_send.at[shift - 1], v_recv.at[shift - 1], {"dp": origin}
        ).wait_recv()
    total = slots[0]
    for k in range(1, dp):
        total = total + slots[k]
    zsend[...] = total

    def sum_copy(shift):
        return remote(
            zsend, zslots.at[my], z_send.at[shift - 1], z_recv.at[shift - 1],
            {"space": sp_peer(shift)},
        )

    for shift in range(1, sp):
        sum_copy(shift).start()
    zslots[my] = total
    for shift in range(1, sp):
        origin = lax.rem(my + sp - shift, sp)
        remote(
            zsend, zslots.at[origin], z_send.at[shift - 1], z_recv.at[shift - 1],
            {"space": origin},
        ).wait_recv()
    total = zslots[0]
    for k in range(1, sp):
        total = total + zslots[k]
    lanes = lax.broadcasted_iota(jnp.int32, (dp, 128), 1)

    def spread(j):
        one = jnp.sum(jnp.where(lanes == j, total, 0.0), axis=1, keepdims=True)
        return jnp.broadcast_to(one, (dp, 128))

    v_t = [spread(j) for j in range(3)]
    v_s = [spread(3 + j) for j in range(3)]
    nu_t = jnp.sqrt(v_t[0] * v_t[0] + v_t[1] * v_t[1] + v_t[2] * v_t[2] + 1e-06)
    nu_s = jnp.sqrt(v_s[0] * v_s[0] + v_s[1] * v_s[1] + v_s[2] * v_s[2] + 1e-06)
    n_s = [v / nu_s for v in v_s]
    diff = [a - b / nu_t for a, b in zip(n_s, v_t)]
    loss = diff[0] * diff[0] + diff[1] * diff[1] + diff[2] * diff[2]
    loss_o[...] = jnp.sum(loss, axis=0, keepdims=True)
    err = [2.0 * d for d in diff]
    along = err[0] * n_s[0] + err[1] * n_s[1] + err[2] * n_s[2]
    for j in range(3):
        coef[j] = (err[j] - along * n_s[j]) / nu_s

    def grad_slice(i):
        one, two = part[0, i], part[1, i]
        weights = (
            2.0 * coef[0, pl.ds(i, 1), :],
            coef[1, pl.ds(i, 1), :] + coef[1, pl.ds(one, 1), :],
            coef[2, pl.ds(i, 1), :] + coef[2, pl.ds(two, 1), :],
        )
        for block in range(chans // 128):
            at = slice(block * 128, (block + 1) * 128)
            own = scut[i, :, at].astype(F32)
            summed = weights[0] * own
            summed = summed + weights[1] * scut[one, :, at].astype(F32)
            summed = summed + weights[2] * scut[two, :, at].astype(F32)
            gcut[i, :, at] = jnp.where(own > 0, elems * summed, 0.0).astype(BF16)

    def grad_copy(shift):
        peer = dp_peer(shift)
        return remote(
            gcut.at[peer], gpre.at[mine], g_send.at[shift - 1], g_recv.at[shift - 1],
            {"dp": peer},
        )

    def send_slice(shift, carry):
        grad_slice(dp_peer(shift))
        grad_copy(shift).start()
        return carry

    lax.fori_loop(1, dp, send_slice, 0)
    grad_slice(me)
    gpre[mine, :] = gcut[me]
    for shift in range(1, dp):
        origin = lax.rem(me + dp - shift, dp)
        remote(
            gcut.at[origin], gpre.at[pl.ds(pl.multiple_of(origin * span, span), span)],
            g_send.at[shift - 1], g_recv.at[shift - 1], {"dp": origin},
        ).wait_recv()

    g2[...] = jnp.where(h2[...] > 0, mm(gpre[...], we[...], 1, 1), 0.0).astype(BF16)
    edges(g2, up2, down2, 2, "start")

    width = chans // sp
    g2t[...] = g2[...].T
    for shift in range(1, sp):
        g2_copy(shift).start()

    def ge_copy(shift):
        return remote(
            gep.at[sp_peer(shift)], ger.at[shift - 1], r_send.at[0, shift - 1],
            r_recv.at[0, shift - 1], {"space": sp_peer(shift)},
        )

    def gr_copy(shift):
        peer = sp_peer(shift)
        return remote(
            grp.at[pl.ds(pl.multiple_of(peer * width, width), width)], grr.at[shift - 1],
            r_send.at[2, shift - 1], r_recv.at[2, shift - 1], {"space": peer},
        )

    for k in range(sp):
        gep[k] = mm(h2t[...], gpre[:, k * width:(k + 1) * width]).astype(BF16)
    for shift in range(1, sp):
        ge_copy(shift).start()
    g2f[my] = g2t[pl.ds(pl.multiple_of(my * depth, depth), depth), :]

    for row in range(rows):
        place(g2[row * cols:(row + 1) * cols, :], row)
    edges(g2, up2, down2, 2, "recv")
    place(up2[...], -1)
    place(down2[...], rows)
    back = None
    for tap in range(9):
        flip = 8 - tap
        term = mm(
            patch[:, tap * mid:(tap + 1) * mid], ws[flip * mid:(flip + 1) * mid, :], 1, 1
        )
        back = term if back is None else back + term
    g1[...] = jnp.where(h1[...] > 0, back, 0.0).astype(BF16)
    grp[...] = mm(xt[...], g1[...]).astype(BF16)
    for shift in range(1, sp):
        gr_copy(shift).start()
    for row in range(rows):
        at = slice(row * cols, (row + 1) * cols)
        gi_o[at, :] = (gpre[at, :].astype(F32) + mm(g1[at, :], wr[...], 1, 1)).astype(BF16)

    for shift in range(1, sp):
        h1_arrival(shift).wait_recv()
        g2_arrival(shift).wait_recv()
    spot = lax.broadcasted_iota(jnp.int32, (depth, cols), 1)
    ahead, centre, behind = [], [], []
    for k in range(sp):
        for row in range(rows):
            piece = g2f[k, :, row * cols:(row + 1) * cols]
            wide = piece.astype(F32)
            ahead.append(
                jnp.where(spot == cols - 1, 0.0, pltpu.roll(wide, cols - 1, 1)).astype(BF16)
            )
            centre.append(piece)
            behind.append(jnp.where(spot == 0, 0.0, pltpu.roll(wide, 1, 1)).astype(BF16))
    stack = jnp.concatenate(
        [jnp.concatenate(line, axis=1) for line in (ahead, centre, behind)], axis=0
    )
    every = sp * pixels
    for a in range(3):
        if a == 0:
            part_sum = mm(stack[:, cols:], h1f[0:every - cols, :])
        elif a == 1:
            part_sum = mm(stack, h1f[...])
        else:
            part_sum = mm(stack[:, :every - cols], h1f[cols:every, :])
        for b in range(3):
            gs_o[a * 3 + b] = part_sum[b * depth:(b + 1) * depth]

    for shift in range(1, sp):
        ge_copy(shift).wait_recv()
    ge = gep[my].astype(F32)
    for k in range(sp - 1):
        ge = ge + ger[k].astype(F32)
    ge_o[...] = ge
    for shift in range(1, sp):
        gr_copy(shift).wait_recv()
    gr = grp[pl.ds(pl.multiple_of(my * width, width), width), :].astype(F32)
    for k in range(sp - 1):
        gr = gr + grr[k].astype(F32)
    gr_o[...] = gr

    for shift in range(1, dp):
        cut_copy(t, tcut, t_send, t_recv, shift).wait_send()
        cut_copy(st, scut, s_send, s_recv, shift).wait_send()
        gram_copy(shift).wait_send()
        grad_copy(shift).wait_send()
    edges(h1, up, down, 0, "send")
    edges(g2, up2, down2, 2, "send")
    for shift in range(1, sp):
        sum_copy(shift).wait_send()
        ge_copy(shift).wait_send()
        h1_copy(shift).wait_send()
        g2_copy(shift).wait_send()
        gr_copy(shift).wait_send()


def body(images, teacher, w_reduce, w_spatial, w_expand, partners):
    dp, sp = lax.axis_size("dp"), lax.axis_size("space")
    _, rows, cols, chans = images.shape
    mid = w_reduce.shape[1]
    pixels = rows * cols
    span, width, depth = pixels // dp, chans // sp, mid // sp
    elems = float(rows * sp * cols * chans)
    vmem = pl.BlockSpec(memory_space=pltpu.VMEM)
    dma = pltpu.SemaphoreType.DMA
    loss, gi, gr, gs, ge = pl.pallas_call(
        functools.partial(kernel, (dp, sp, rows, cols, elems)),
        out_shape=(
            jax.ShapeDtypeStruct((1, 128), F32),
            jax.ShapeDtypeStruct((pixels, chans), BF16),
            jax.ShapeDtypeStruct((width, mid), F32),
            jax.ShapeDtypeStruct((9, depth, mid), F32),
            jax.ShapeDtypeStruct((mid, width), F32),
        ),
        in_specs=[pl.BlockSpec(memory_space=pltpu.SMEM)] + [pl.BlockSpec(memory_space=pl.ANY)] * 5,
        out_specs=(vmem,) * 5,
        scratch_shapes=[
            pltpu.VMEM((pixels, chans), BF16),
            pltpu.VMEM((chans, mid), BF16),
            pltpu.VMEM((9 * mid, mid), BF16),
            pltpu.VMEM((mid, chans), BF16),
            pltpu.VMEM((pixels, mid), BF16),
            pltpu.VMEM((pixels, mid), BF16),
            pltpu.VMEM((sp * pixels, mid), BF16),
            pltpu.VMEM((mid, pixels), BF16),
            pltpu.VMEM((sp, depth, pixels), BF16),
            pltpu.VMEM((pixels, mid), BF16),
            pltpu.VMEM((pixels, chans), BF16),
            pltpu.VMEM((pixels, 9 * mid), BF16),
            pltpu.VMEM((pixels, mid), BF16),
            pltpu.VMEM((chans, pixels), BF16),
            pltpu.VMEM((mid, pixels), BF16),
            pltpu.VMEM((cols, mid), BF16),
            pltpu.VMEM((cols, mid), BF16),
            pltpu.VMEM((cols, mid), BF16),
            pltpu.VMEM((cols, mid), BF16),
            pltpu.VMEM((dp, span, chans), BF16),
            pltpu.VMEM((dp, span, chans), BF16),
            pltpu.VMEM((dp, span, chans), BF16),
            pltpu.VMEM((pixels, chans), BF16),
            pltpu.VMEM((dp, 128), F32),
            pltpu.VMEM((dp, dp, 128), F32),
            pltpu.VMEM((dp, 128), F32),
            pltpu.VMEM((sp, dp, 128), F32),
            pltpu.VMEM((3, dp, 128), F32),
            pltpu.VMEM((chans, mid), BF16),
            pltpu.VMEM((sp, mid, width), BF16),
            pltpu.VMEM((sp - 1, width, mid), BF16),
            pltpu.VMEM((sp - 1, mid, width), BF16),
            dma((dp - 1,)), dma((dp - 1,)), dma((dp - 1,)), dma((dp - 1,)),
            dma((dp - 1,)), dma((dp - 1,)), dma((dp - 1,)), dma((dp - 1,)),
            dma((sp - 1,)), dma((sp - 1,)), dma((4,)), dma((4,)),
            dma((4, sp - 1)), dma((4, sp - 1)), dma((5,)),
        ],
        compiler_params=pltpu.CompilerParams(
            collective_id=0, has_side_effects=True, vmem_limit_bytes=48 * 1024 * 1024
        ),
        name="distill",
    )(
        partners,
        images.reshape(pixels, chans),
        teacher.reshape(pixels, chans),
        w_reduce,
        w_spatial.reshape(9 * mid, mid),
        w_expand,
    )
    return (
        loss[0, 0],
        gi.reshape(images.shape),
        gr[None],
        gs.reshape(1, 3, 3, depth, mid).transpose(0, 1, 2, 4, 3),
        ge[None],
    )


def solution(mesh):
    return jax.shard_map(
        body,
        mesh=mesh,
        in_specs=(P("dp", "space", None, None), P("dp", "space", None, None), P(), P(), P(), P()),
        out_specs=(
            P(),
            P("dp", "space", None, None),
            P("dp", "space", None),
            P("dp", None, None, None, "space"),
            P("dp", None, "space"),
        ),
        check_vma=False,
    )
```

```python
import functools

import jax
import jax.numpy as jnp
from jax import lax
from jax.experimental import pallas as pl
from jax.experimental.pallas import tpu as pltpu
from jax.sharding import PartitionSpec as P

MESH = pl.DeviceIdType.MESH
F32 = jnp.float32
BF16 = jnp.bfloat16


def mm(a, b, ca=1, cb=0):
    return lax.dot_general(a, b, (((ca,), (cb,)), ((), ())), preferred_element_type=F32)


def kernel(
    dims, part, x_hbm, t, wr_hbm, ws_hbm, we_hbm,
    loss_o, gi_o, gr_o, gs_o, ge_o,
    x, wr, ws, we, h1, g1, h1f, g2t, g2f, h2, st, patch, g2, xt, h2t, up, down, up2, down2,
    tcut, scut, gcut, gpre, gram, slots, zsend, zslots, coef,
    grp, gep, grr, ger,
    t_send, t_recv, s_send, s_recv, g_send, g_recv, v_send, v_recv,
    z_send, z_recv, e_send, e_recv, r_send, r_recv, l_sem,
):
    dp, sp, rows, cols, elems = dims
    chans, mid = wr_hbm.shape
    pixels = rows * cols
    span = pixels // dp
    me = lax.axis_index("dp")
    my = lax.axis_index("space")

    def dp_peer(shift):
        return lax.rem(me + shift, dp)

    def sp_peer(shift):
        return lax.rem(my + shift, sp)

    def remote(src, dst, send, recv, where):
        return pltpu.make_async_remote_copy(
            src_ref=src, dst_ref=dst, send_sem=send, recv_sem=recv,
            device_id=where, device_id_type=MESH,
        )

    loads = [
        pltpu.make_async_copy(src, dst, l_sem.at[k])
        for k, (src, dst) in enumerate(((x_hbm, x), (wr_hbm, wr), (ws_hbm, ws), (we_hbm, we)))
    ]
    for load in loads:
        load.start()
    up[...] = jnp.zeros_like(up)
    down[...] = jnp.zeros_like(down)
    up2[...] = jnp.zeros_like(up2)
    down2[...] = jnp.zeros_like(down2)

    barrier = pltpu.get_barrier_semaphore()
    for shift in range(1, dp):
        pl.semaphore_signal(
            barrier, inc=1, device_id={"dp": dp_peer(shift)}, device_id_type=MESH
        )
    for shift in range(1, sp):
        pl.semaphore_signal(
            barrier, inc=1, device_id={"space": sp_peer(shift)}, device_id_type=MESH
        )
    pl.semaphore_wait(barrier, dp + sp - 2)

    def cut_copy(src, dst, send, recv, shift):
        peer = dp_peer(shift)
        return remote(
            src.at[pl.ds(pl.multiple_of(peer * span, span), span)],
            dst.at[me], send.at[shift - 1], recv.at[shift - 1], {"dp": peer},
        )

    def cut_arrival(src, dst, send, recv, shift):
        origin = lax.rem(me + dp - shift, dp)
        return remote(
            src.at[pl.ds(0, span)], dst.at[origin],
            send.at[shift - 1], recv.at[shift - 1], {"dp": origin},
        )

    mine = pl.ds(pl.multiple_of(me * span, span), span)
    for shift in range(1, dp):
        cut_copy(t, tcut, t_send, t_recv, shift).start()
    own_cut = pltpu.make_async_copy(t.at[mine], tcut.at[me], l_sem.at[4])
    own_cut.start()

    def edges(src, above, below, base, act):
        first, last = src.at[pl.ds(0, cols)], src.at[pl.ds(pixels - cols, cols)]

        def move(part_rows, dst, slot, peer):
            return remote(
                part_rows, dst, e_send.at[slot], e_recv.at[slot], {"space": peer}
            )

        @pl.when(my > 0)
        def _():
            if act == "start":
                move(first, below, base, my - 1).start()
            elif act == "recv":
                move(first, above, base + 1, my - 1).wait_recv()
            else:
                move(first, below, base, my - 1).wait_send()

        @pl.when(my < sp - 1)
        def _():
            if act == "start":
                move(last, above, base + 1, my + 1).start()
            elif act == "recv":
                move(last, below, base, my + 1).wait_recv()
            else:
                move(last, above, base + 1, my + 1).wait_send()

    column = lax.broadcasted_iota(jnp.int32, (cols, mid), 0)

    def place(value, row):
        wide = value.astype(F32)
        left = jnp.where(column == 0, 0.0, pltpu.roll(wide, 1, 0)).astype(BF16)
        right = jnp.where(column == cols - 1, 0.0, pltpu.roll(wide, cols - 1, 0)).astype(BF16)
        for a in range(3):
            to = row - a + 1
            if 0 <= to < rows:
                for b, piece in enumerate((left, value, right)):
                    tap = a * 3 + b
                    patch[to * cols:(to + 1) * cols, tap * mid:(tap + 1) * mid] = piece

    depth = mid // sp

    def h1_copy(shift):
        return remote(
            h1, h1f.at[pl.ds(pl.multiple_of(my * pixels, pixels), pixels)],
            r_send.at[1, shift - 1], r_recv.at[1, shift - 1], {"space": sp_peer(shift)},
        )

    def h1_arrival(shift):
        origin = lax.rem(my + sp - shift, sp)
        return remote(
            h1, h1f.at[pl.ds(pl.multiple_of(origin * pixels, pixels), pixels)],
            r_send.at[1, shift - 1], r_recv.at[1, shift - 1], {"space": origin},
        )

    def g2_copy(shift):
        peer = sp_peer(shift)
        return remote(
            g2t.at[pl.ds(pl.multiple_of(peer * depth, depth), depth)], g2f.at[my],
            r_send.at[3, shift - 1], r_recv.at[3, shift - 1], {"space": peer},
        )

    def g2_arrival(shift):
        origin = lax.rem(my + sp - shift, sp)
        return remote(
            g2t.at[pl.ds(0, depth)], g2f.at[origin],
            r_send.at[3, shift - 1], r_recv.at[3, shift - 1], {"space": origin},
        )

    loads[0].wait()
    loads[1].wait()
    h1[...] = jnp.maximum(mm(x[...], wr[...]), 0.0).astype(BF16)
    edges(h1, up, down, 0, "start")
    for shift in range(1, sp):
        h1_copy(shift).start()
    h1f[pl.ds(pl.multiple_of(my * pixels, pixels), pixels), :] = h1[...]
    for row in range(rows):
        place(h1[row * cols:(row + 1) * cols, :], row)
    edges(h1, up, down, 0, "recv")
    place(up[...], -1)
    place(down[...], rows)
    loads[2].wait()
    loads[3].wait()
    h2[...] = jnp.maximum(mm(patch[...], ws[...]), 0.0).astype(BF16)
    for row in range(rows):
        at = slice(row * cols, (row + 1) * cols)
        st[at, :] = jnp.maximum(mm(h2[at, :], we[...]) + x[at, :].astype(F32), 0.0).astype(BF16)
    for shift in range(1, dp):
        cut_copy(st, scut, s_send, s_recv, shift).start()
    scut[me] = st[mine, :]

    lane = lax.broadcasted_iota(jnp.int32, (1, 128), 1)

    def gram_rows(cut, first):
        def one(i, carry):
            others = [part[0, i], part[1, i]]
            sums = [jnp.zeros((8, 128), F32) for _ in range(3)]
            for block in range(chans // 128):
                at = slice(block * 128, (block + 1) * 128)
                own = cut[i, :, at].astype(F32)
                for j, right in enumerate(
                    (own, cut[others[0], :, at].astype(F32), cut[others[1], :, at].astype(F32))
                ):
                    sums[j] = sums[j] + jnp.sum((own * right).reshape(span // 8, 8, 128), axis=0)
            line = jnp.zeros((1, 128), F32)
            for j in range(3):
                total = jnp.sum(jnp.sum(sums[j], axis=0, keepdims=True), axis=1, keepdims=True)
                line = jnp.where(lane == first + j, total, line)
            if first:
                gram[pl.ds(i, 1), :] = jnp.where(lane >= first, line, gram[pl.ds(i, 1), :])
            else:
                gram[pl.ds(i, 1), :] = line
            return carry

        lax.fori_loop(0, dp, one, 0)

    for shift in range(1, dp):
        cut_arrival(t, tcut, t_send, t_recv, shift).wait_recv()
    own_cut.wait()
    gram_rows(tcut, 0)
    xt[...] = x[...].T
    h2t[...] = h2[...].T
    for shift in range(1, dp):
        cut_arrival(st, scut, s_send, s_recv, shift).wait_recv()
    gram_rows(scut, 3)

    def gram_copy(shift):
        return remote(
            gram, slots.at[me], v_send.at[shift - 1], v_recv.at[shift - 1],
            {"dp": dp_peer(shift)},
        )

    for shift in range(1, dp):
        gram_copy(shift).start()
    slots[me] = gram[...]
    for shift in range(1, dp):
        origin = lax.rem(me + dp - shift, dp)
        remote(
            gram, slots.at[origin], v_send.at[shift - 1], v_recv.at[shift - 1], {"dp": origin}
        ).wait_recv()
    total = slots[0]
    for k in range(1, dp):
        total = total + slots[k]
    zsend[...] = total

    def sum_copy(shift):
        return remote(
            zsend, zslots.at[my], z_send.at[shift - 1], z_recv.at[shift - 1],
            {"space": sp_peer(shift)},
        )

    for shift in range(1, sp):
        sum_copy(shift).start()
    zslots[my] = total
    for shift in range(1, sp):
        origin = lax.rem(my + sp - shift, sp)
        remote(
            zsend, zslots.at[origin], z_send.at[shift - 1], z_recv.at[shift - 1],
            {"space": origin},
        ).wait_recv()
    total = zslots[0]
    for k in range(1, sp):
        total = total + zslots[k]
    lanes = lax.broadcasted_iota(jnp.int32, (dp, 128), 1)

    def spread(j):
        one = jnp.sum(jnp.where(lanes == j, total, 0.0), axis=1, keepdims=True)
        return jnp.broadcast_to(one, (dp, 128))

    v_t = [spread(j) for j in range(3)]
    v_s = [spread(3 + j) for j in range(3)]
    nu_t = jnp.sqrt(v_t[0] * v_t[0] + v_t[1] * v_t[1] + v_t[2] * v_t[2] + 1e-06)
    nu_s = jnp.sqrt(v_s[0] * v_s[0] + v_s[1] * v_s[1] + v_s[2] * v_s[2] + 1e-06)
    n_s = [v / nu_s for v in v_s]
    diff = [a - b / nu_t for a, b in zip(n_s, v_t)]
    loss = diff[0] * diff[0] + diff[1] * diff[1] + diff[2] * diff[2]
    loss_o[...] = jnp.sum(loss, axis=0, keepdims=True)
    err = [2.0 * d for d in diff]
    along = err[0] * n_s[0] + err[1] * n_s[1] + err[2] * n_s[2]
    for j in range(3):
        coef[j] = (err[j] - along * n_s[j]) / nu_s

    def grad_slice(i):
        one, two = part[0, i], part[1, i]
        weights = (
            2.0 * coef[0, pl.ds(i, 1), :],
            coef[1, pl.ds(i, 1), :] + coef[1, pl.ds(one, 1), :],
            coef[2, pl.ds(i, 1), :] + coef[2, pl.ds(two, 1), :],
        )
        for block in range(chans // 128):
            at = slice(block * 128, (block + 1) * 128)
            own = scut[i, :, at].astype(F32)
            summed = weights[0] * own
            summed = summed + weights[1] * scut[one, :, at].astype(F32)
            summed = summed + weights[2] * scut[two, :, at].astype(F32)
            gcut[i, :, at] = jnp.where(own > 0, elems * summed, 0.0).astype(BF16)

    def grad_copy(shift):
        peer = dp_peer(shift)
        return remote(
            gcut.at[peer], gpre.at[mine], g_send.at[shift - 1], g_recv.at[shift - 1],
            {"dp": peer},
        )

    def send_slice(shift, carry):
        grad_slice(dp_peer(shift))
        grad_copy(shift).start()
        return carry

    lax.fori_loop(1, dp, send_slice, 0)
    grad_slice(me)
    gpre[mine, :] = gcut[me]
    for shift in range(1, dp):
        origin = lax.rem(me + dp - shift, dp)
        remote(
            gcut.at[origin], gpre.at[pl.ds(pl.multiple_of(origin * span, span), span)],
            g_send.at[shift - 1], g_recv.at[shift - 1], {"dp": origin},
        ).wait_recv()

    g2[...] = jnp.where(h2[...] > 0, mm(gpre[...], we[...], 1, 1), 0.0).astype(BF16)
    edges(g2, up2, down2, 2, "start")

    width = chans // sp
    g2t[...] = g2[...].T
    for shift in range(1, sp):
        g2_copy(shift).start()

    def ge_copy(shift):
        return remote(
            gep.at[sp_peer(shift)], ger.at[shift - 1], r_send.at[0, shift - 1],
            r_recv.at[0, shift - 1], {"space": sp_peer(shift)},
        )

    def gr_copy(shift):
        peer = sp_peer(shift)
        return remote(
            grp.at[pl.ds(pl.multiple_of(peer * width, width), width)], grr.at[shift - 1],
            r_send.at[2, shift - 1], r_recv.at[2, shift - 1], {"space": peer},
        )

    for k in range(sp):
        gep[k] = mm(h2t[...], gpre[:, k * width:(k + 1) * width]).astype(BF16)
    for shift in range(1, sp):
        ge_copy(shift).start()
    g2f[my] = g2t[pl.ds(pl.multiple_of(my * depth, depth), depth), :]

    for row in range(rows):
        place(g2[row * cols:(row + 1) * cols, :], row)
    edges(g2, up2, down2, 2, "recv")
    place(up2[...], -1)
    place(down2[...], rows)
    back = None
    for tap in range(9):
        flip = 8 - tap
        term = mm(
            patch[:, tap * mid:(tap + 1) * mid], ws[flip * mid:(flip + 1) * mid, :], 1, 1
        )
        back = term if back is None else back + term
    g1[...] = jnp.where(h1[...] > 0, back, 0.0).astype(BF16)
    grp[...] = mm(xt[...], g1[...]).astype(BF16)
    for shift in range(1, sp):
        gr_copy(shift).start()
    for row in range(rows):
        at = slice(row * cols, (row + 1) * cols)
        gi_o[at, :] = (gpre[at, :].astype(F32) + mm(g1[at, :], wr[...], 1, 1)).astype(BF16)

    for shift in range(1, sp):
        h1_arrival(shift).wait_recv()
        g2_arrival(shift).wait_recv()
    spot = lax.broadcasted_iota(jnp.int32, (depth, cols), 1)
    ahead, centre, behind = [], [], []
    for k in range(sp):
        for row in range(rows):
            piece = g2f[k, :, row * cols:(row + 1) * cols]
            wide = piece.astype(F32)
            ahead.append(
                jnp.where(spot == cols - 1, 0.0, pltpu.roll(wide, cols - 1, 1)).astype(BF16)
            )
            centre.append(piece)
            behind.append(jnp.where(spot == 0, 0.0, pltpu.roll(wide, 1, 1)).astype(BF16))
    stack = jnp.concatenate(
        [jnp.concatenate(line, axis=1) for line in (ahead, centre, behind)], axis=0
    )
    every = sp * pixels
    for a in range(3):
        if a == 0:
            part_sum = mm(stack[:, cols:], h1f[0:every - cols, :])
        elif a == 1:
            part_sum = mm(stack, h1f[...])
        else:
            part_sum = mm(stack[:, :every - cols], h1f[cols:every, :])
        for b in range(3):
            gs_o[a * 3 + b] = part_sum[b * depth:(b + 1) * depth]

    for shift in range(1, sp):
        ge_copy(shift).wait_recv()
    ge = gep[my].astype(F32)
    for k in range(sp - 1):
        ge = ge + ger[k].astype(F32)
    ge_o[...] = ge
    for shift in range(1, sp):
        gr_copy(shift).wait_recv()
    gr = grp[pl.ds(pl.multiple_of(my * width, width), width), :].astype(F32)
    for k in range(sp - 1):
        gr = gr + grr[k].astype(F32)
    gr_o[...] = gr

    for shift in range(1, dp):
        cut_copy(t, tcut, t_send, t_recv, shift).wait_send()
        cut_copy(st, scut, s_send, s_recv, shift).wait_send()
        gram_copy(shift).wait_send()
        grad_copy(shift).wait_send()
    edges(h1, up, down, 0, "send")
    edges(g2, up2, down2, 2, "send")
    for shift in range(1, sp):
        sum_copy(shift).wait_send()
        ge_copy(shift).wait_send()
        h1_copy(shift).wait_send()
        g2_copy(shift).wait_send()
        gr_copy(shift).wait_send()


def body(images, teacher, w_reduce, w_spatial, w_expand, partners):
    dp, sp = lax.axis_size("dp"), lax.axis_size("space")
    _, rows, cols, chans = images.shape
    mid = w_reduce.shape[1]
    pixels = rows * cols
    span, width, depth = pixels // dp, chans // sp, mid // sp
    elems = float(rows * sp * cols * chans)
    vmem = pl.BlockSpec(memory_space=pltpu.VMEM)
    dma = pltpu.SemaphoreType.DMA
    loss, gi, gr, gs, ge = pl.pallas_call(
        functools.partial(kernel, (dp, sp, rows, cols, elems)),
        out_shape=(
            jax.ShapeDtypeStruct((1, 128), F32),
            jax.ShapeDtypeStruct((pixels, chans), BF16),
            jax.ShapeDtypeStruct((width, mid), F32),
            jax.ShapeDtypeStruct((9, depth, mid), F32),
            jax.ShapeDtypeStruct((mid, width), F32),
        ),
        in_specs=[pl.BlockSpec(memory_space=pltpu.SMEM)] + [pl.BlockSpec(memory_space=pl.ANY)] * 5,
        out_specs=(vmem,) * 5,
        scratch_shapes=[
            pltpu.VMEM((pixels, chans), BF16),
            pltpu.VMEM((chans, mid), BF16),
            pltpu.VMEM((9 * mid, mid), BF16),
            pltpu.VMEM((mid, chans), BF16),
            pltpu.VMEM((pixels, mid), BF16),
            pltpu.VMEM((pixels, mid), BF16),
            pltpu.VMEM((sp * pixels, mid), BF16),
            pltpu.VMEM((mid, pixels), BF16),
            pltpu.VMEM((sp, depth, pixels), BF16),
            pltpu.VMEM((pixels, mid), BF16),
            pltpu.VMEM((pixels, chans), BF16),
            pltpu.VMEM((pixels, 9 * mid), BF16),
            pltpu.VMEM((pixels, mid), BF16),
            pltpu.VMEM((chans, pixels), BF16),
            pltpu.VMEM((mid, pixels), BF16),
            pltpu.VMEM((cols, mid), BF16),
            pltpu.VMEM((cols, mid), BF16),
            pltpu.VMEM((cols, mid), BF16),
            pltpu.VMEM((cols, mid), BF16),
            pltpu.VMEM((dp, span, chans), BF16),
            pltpu.VMEM((dp, span, chans), BF16),
            pltpu.VMEM((dp, span, chans), BF16),
            pltpu.VMEM((pixels, chans), BF16),
            pltpu.VMEM((dp, 128), F32),
            pltpu.VMEM((dp, dp, 128), F32),
            pltpu.VMEM((dp, 128), F32),
            pltpu.VMEM((sp, dp, 128), F32),
            pltpu.VMEM((3, dp, 128), F32),
            pltpu.VMEM((chans, mid), BF16),
            pltpu.VMEM((sp, mid, width), BF16),
            pltpu.VMEM((sp - 1, width, mid), BF16),
            pltpu.VMEM((sp - 1, mid, width), BF16),
            dma((dp - 1,)), dma((dp - 1,)), dma((dp - 1,)), dma((dp - 1,)),
            dma((dp - 1,)), dma((dp - 1,)), dma((dp - 1,)), dma((dp - 1,)),
            dma((sp - 1,)), dma((sp - 1,)), dma((4,)), dma((4,)),
            dma((4, sp - 1)), dma((4, sp - 1)), dma((5,)),
        ],
        compiler_params=pltpu.CompilerParams(
            collective_id=0, has_side_effects=True, vmem_limit_bytes=60 * 1024 * 1024
        ),
        name="distill",
    )(
        partners,
        images.reshape(pixels, chans),
        teacher.reshape(pixels, chans),
        w_reduce,
        w_spatial.reshape(9 * mid, mid),
        w_expand,
    )
    return (
        loss[0, 0],
        gi.reshape(images.shape),
        gr[None],
        gs.reshape(1, 3, 3, depth, mid).transpose(0, 1, 2, 4, 3),
        ge[None],
    )


def solution(mesh):
    return jax.shard_map(
        body,
        mesh=mesh,
        in_specs=(P("dp", "space", None, None), P("dp", "space", None, None), P(), P(), P(), P()),
        out_specs=(
            P(),
            P("dp", "space", None, None),
            P("dp", "space", None),
            P("dp", None, None, None, "space"),
            P("dp", None, "space"),
        ),
        check_vma=False,
    )
```
